32 devices in a mesh: blk: 8 (over z, y), head: 4 (over x, core).
Axes of the slice: x: 2, y: 2, z: 4, core: 2. Of those that a mesh axis runs over, the one named last changes fastest.
Arguments:
- queries: bfloat16 [2048, 8192], P(('blk', 'head')), may hold values from -6 to 6
- keys: bfloat16 [2048, 1024], P(('blk', 'head')), may hold values from -6 to 6
- values: bfloat16 [2048, 1024], P(('blk', 'head')), may hold values from -6 to 6
- doc_lengths: int32 [6], replicated, may hold values from 1 to 1024, 2048 in all
- stored_block_order: int32 [16], replicated, may hold values from 0 to 15, each once
Outputs:
- attended: bfloat16 [2048, 8192], P(('blk', 'head'))
The draws below stay inside these ranges and needn't reach their ends.
Inputs may be any that keep to these rules, and one draw needn't show every extreme that they name: `stored_block_order`: each stored block holds a different prompt block.
All inputs are finite; a program needn't handle non-finite values.
Results may differ from the reference program's by a relative error of at most 0.0034.
Values may be sent and summed in bfloat16 or wider, within the bound.
A program may use at most 64 MiB of HBM per device.

```python
import math
import jax
import jax.numpy as jnp
import numpy as np
from jax import lax

QUERY_HEADS = 64
KEY_VALUE_HEADS = 8
HEAD_WIDTH = 128
DOCS = 6
PROMPT_TOKENS = 2048
PROMPT_BLOCKS = 16


def draw_queries(key, part):
    key = jax.random.fold_in(key, 1)
    first_part = jax.random.fold_in(key, 0)
    base_offset = jax.random.truncated_normal(first_part, -6.0, 6.0, (PROMPT_TOKENS, QUERY_HEADS, HEAD_WIDTH), jnp.float32)
    return base_offset.reshape(PROMPT_TOKENS, QUERY_HEADS * HEAD_WIDTH).astype(jnp.bfloat16)


def draw_keys(key, part):
    key = jax.random.fold_in(key, 2)
    first_part = jax.random.fold_in(key, 0)
    base_offset = jax.random.truncated_normal(first_part, -6.0, 6.0, (PROMPT_TOKENS, KEY_VALUE_HEADS, HEAD_WIDTH), jnp.float32)
    return base_offset.reshape(PROMPT_TOKENS, KEY_VALUE_HEADS * HEAD_WIDTH).astype(jnp.bfloat16)


def steps_of(rng, extent, cuts, least, top_value):
    def one(position, shards_of):
        steps = jax.random.uniform(jax.random.fold_in(jax.random.fold_in(rng, 6), position), (shards_of,), jnp.float32, least / len(cuts), top_value / len(cuts))
        return jnp.repeat(jnp.exp(steps), extent[position] // shards_of).reshape((-1,) + (1,) * (len(extent) - position - 1))

    factor_of = one(*cuts[0])
    for cut in cuts[1:]:
        factor_of = factor_of * one(*cut)
    return factor_of


def split_up(number_of, total, reach, skew):
    portions = [(1 << 20) // math.isqrt(grade ** skew) + 1 for grade in range(2, number_of + 1)]
    rest, holding = total - reach - (number_of - 1), [1] * (number_of - 1)
    while rest > 0:
        free = [i for i in range(number_of - 1) if holding[i] < reach]
        whole, remaining = sum([portions[i] for i in free]), rest
        for i in free:
            addition = min(reach - holding[i], max(1, remaining * portions[i] // whole), rest)
            holding[i] = holding[i] + addition
            rest = rest - addition
    return np.array([reach] + holding)


def ragged_sizes(rng, amount, total, most, slope):
    if amount == 2:
        one = jax.random.randint(rng, (), max(1, total - most), min(most, total - 1) + 1)
        return jnp.stack([one, total - one])
    lengths = jnp.asarray(split_up(amount, total, most, slope), jnp.int32)
    couples = (amount - 1) // 2
    donor, sink = lengths[1:1 + 2 * couples:2], lengths[2:2 + 2 * couples:2]
    margin = jnp.minimum(donor - 1, most - sink)
    shifted = jax.random.randint(jax.random.fold_in(rng, 1), (couples,), 0, 1 << 20) % (margin + 1)
    lengths = lengths.at[1:1 + 2 * couples:2].set(donor - shifted).at[2:2 + 2 * couples:2].set(sink + shifted)
    return lengths[jax.random.permutation(jax.random.fold_in(rng, 2), amount)]


def normal_values(stream_key, extent, width, limit, cuts=(), kind=jnp.bfloat16):
    result = jax.random.normal(stream_key, extent, jnp.float32) * width
    if len(cuts) > 0:
        result = steps_of(stream_key, extent, cuts, -0.22, 0.18) * result
    return jnp.clip(result, min=-limit, max=limit).astype(kind)


def setup_inputs(seed: int = 0) -> dict:
    streams_of = jax.random.split(jax.random.key(seed), 6)
    return {
        "queries": draw_queries(jax.random.fold_in(streams_of[5], 71), 0),
        "keys": draw_keys(jax.random.fold_in(streams_of[5], 71), 0),
        "values": normal_values(streams_of[2], (PROMPT_TOKENS, KEY_VALUE_HEADS * HEAD_WIDTH), 1.0, 6.0, ((0, 32),)),
        "doc_lengths": ragged_sizes(streams_of[3], DOCS, PROMPT_TOKENS, PROMPT_TOKENS // 2, 2).astype(jnp.int32),
        "stored_block_order": jax.random.permutation(streams_of[4], PROMPT_BLOCKS).astype(jnp.int32),
    }


def reference(queries, keys, values, doc_lengths, stored_block_order):
    token_length = queries.shape[0]
    block_count = stored_block_order.shape[0]
    block_length = token_length // block_count
    idx = jnp.arange(token_length, dtype=jnp.int32)
    orig = stored_block_order[idx // block_length] * block_length + idx % block_length
    ends = jnp.cumsum(doc_lengths).astype(jnp.int32)
    docs = jnp.sum((orig[:, None] >= ends[None, :]).astype(jnp.int32), axis=1)
    allowed = (orig[None, :] <= orig[:, None]) & (docs[None, :] == docs[:, None])
    head_ratio = QUERY_HEADS // KEY_VALUE_HEADS
    qs = jnp.transpose(queries.reshape(token_length, QUERY_HEADS, HEAD_WIDTH), (1, 0, 2))
    key_tensor = jnp.transpose(keys.reshape(token_length, KEY_VALUE_HEADS, HEAD_WIDTH), (1, 0, 2))
    value_tensor = jnp.transpose(values.reshape(token_length, KEY_VALUE_HEADS, HEAD_WIDTH), (1, 0, 2))
    scale = HEAD_WIDTH ** -0.5

    def one_head(item):
        query_head, number = item
        group = (number // head_ratio).astype(jnp.int32)
        key_head = lax.dynamic_index_in_dim(key_tensor, group, 0, keepdims=False)
        value_head = lax.dynamic_index_in_dim(value_tensor, group, 0, keepdims=False)
        scores = jnp.dot(query_head, key_head.T, preferred_element_type=jnp.float32) * scale
        scores = jnp.where(allowed, scores, -1e30)
        top = jnp.max(scores, axis=1, keepdims=True)
        weights = jnp.where(allowed, jnp.exp(scores - top), 0.0)
        total = jnp.sum(weights, axis=1, keepdims=True)
        mixed = jnp.dot(weights.astype(jnp.bfloat16), value_head, preferred_element_type=jnp.float32)
        return mixed / total

    outs = lax.map(one_head, (qs, jnp.arange(QUERY_HEADS, dtype=jnp.int32)))
    return jnp.transpose(outs, (1, 0, 2)).reshape(token_length, QUERY_HEADS * HEAD_WIDTH).astype(jnp.bfloat16)
```

```python
import functools
import math

import jax
import jax.numpy as jnp
from jax import lax
from jax.experimental import pallas as pl
from jax.experimental.pallas import tpu as pltpu
from jax.sharding import PartitionSpec as P

HEAD_WIDTH = 128
LANES = 128
SCORE_TO_LOG2 = HEAD_WIDTH ** (-0.5) * math.log2(math.e)
MASKED = -1e30
START_TOP = -1e25
F32 = jnp.float32
BF16 = jnp.bfloat16
MESH = pl.DeviceIdType.MESH


def query_limits(lengths_ref, order_ref, first_row, rows, block_length):
    lane = lax.broadcasted_iota(jnp.int32, (1, LANES), 1) % rows
    slot = first_row // block_length
    pos = order_ref[slot] * block_length + first_row % block_length + lane
    begin = jnp.zeros_like(pos)
    end = jnp.int32(0)
    for i in range(lengths_ref.shape[0]):
        end = end + lengths_ref[i]
        begin = jnp.where(pos >= end, end, begin)
    return pos, begin


def fill_bias(bias_ref, order_ref, first_slot, pos, begin, block_length):
    for j in range(bias_ref.shape[0] // block_length):
        key = (
            order_ref[first_slot + j] * block_length
            + lax.broadcasted_iota(jnp.int32, (block_length, LANES), 0)
        )
        allowed = (key <= pos) & (key >= begin)
        bias_ref[j * block_length : (j + 1) * block_length, :] = jnp.where(
            allowed, 0.0, MASKED
        ).astype(F32)


def stack_queries(g, q_ref, qt_ref, ratio):
    heads = [
        q_ref[:, pl.ds(pl.multiple_of((g * ratio + j) * HEAD_WIDTH, HEAD_WIDTH), HEAD_WIDTH)]
        for j in range(ratio)
    ]
    qt_ref[g] = jnp.concatenate(heads, axis=0).T


def attend(g, k, v, qt_ref, bias_ref, top_ref, total_ref, accum_ref):
    width = qt_ref.shape[2]
    scores = jnp.dot(k, qt_ref[g], preferred_element_type=F32)
    scores = scores + jnp.concatenate([bias_ref[...]] * (width // LANES), axis=1)
    top = top_ref[g]
    new_top = jnp.maximum(top, jnp.max(scores, axis=0, keepdims=True))
    weights = jnp.exp2((scores - new_top) * SCORE_TO_LOG2)
    factor = jnp.exp2((top - new_top) * SCORE_TO_LOG2)
    top_ref[g] = new_top
    total_ref[g] = total_ref[g] * factor + jnp.sum(weights, axis=0, keepdims=True)
    accum_ref[g] = accum_ref[g] * factor + jnp.dot(
        v.T, weights.astype(BF16), preferred_element_type=F32
    )


def finish(g, out_ref, total_ref, accum_ref, rows, ratio):
    result = (accum_ref[g] / total_ref[g]).T.astype(BF16)
    for j in range(ratio):
        cols = pl.ds(pl.multiple_of((g * ratio + j) * HEAD_WIDTH, HEAD_WIDTH), HEAD_WIDTH)
        out_ref[:, cols] = result[j * rows : (j + 1) * rows]


def reset(top_ref, total_ref, accum_ref):
    top_ref[...] = jnp.full(top_ref.shape, START_TOP, F32)
    total_ref[...] = jnp.zeros(total_ref.shape, F32)
    accum_ref[...] = jnp.zeros(accum_ref.shape, F32)


def head_columns(g):
    return pl.ds(pl.multiple_of(g * HEAD_WIDTH, HEAD_WIDTH), HEAD_WIDTH)


def chunk_kernel(ratio, block_length, first_ref, lengths_ref, order_ref, q_ref, k_ref, v_ref,
                 out_ref, qt_ref, bias_ref, top_ref, total_ref, accum_ref):
    step = pl.program_id(0)
    rows = q_ref.shape[0]
    groups = k_ref.shape[1] // HEAD_WIDTH
    chunk = k_ref.shape[0]

    @pl.when(step == 0)
    def _():
        reset(top_ref, total_ref, accum_ref)
        pl.loop(0, groups)(lambda g: stack_queries(g, q_ref, qt_ref, ratio))

    pos, begin = query_limits(lengths_ref, order_ref, first_ref[0], rows, block_length)
    fill_bias(bias_ref, order_ref, step * (chunk // block_length), pos, begin, block_length)

    @pl.loop(0, groups)
    def _(g):
        attend(g, k_ref[:, head_columns(g)], v_ref[:, head_columns(g)],
               qt_ref, bias_ref, top_ref, total_ref, accum_ref)

    @pl.when(step == pl.num_programs(0) - 1)
    def _():
        pl.loop(0, groups)(lambda g: finish(g, out_ref, total_ref, accum_ref, rows, ratio))


def gather_kernel(ratio, block_length, lengths_ref, order_ref, q_hbm, k_hbm, v_hbm, out_ref,
                  q_ref, k_buf, v_buf, qt_ref, bias_ref, top_ref, total_ref, accum_ref,
                  local_sem, k_recv, v_recv, k_send, v_send):
    rows, width = k_hbm.shape
    groups = width // HEAD_WIDTH
    blk, head = lax.axis_index("blk"), lax.axis_index("head")
    z, y, x, c = blk // 2, blk % 2, head // 2, head % 2
    me = blk * 4 + head
    hi = z // 2
    zz = z + hi * (3 - 2 * z)

    def flip(f):
        return f + hi * (3 - 2 * f)

    def plane(i):
        return flip(i + zz * (1 - 2 * i)) if i < 2 else flip(i)

    def shard(p, dy, dx, dc=0):
        yy = y + dy * (1 - 2 * y)
        xx = x + dx * (1 - 2 * x)
        cc = c + dc * (1 - 2 * c)
        return ((p * 2 + yy) * 2 + xx) * 2 + cc

    sibling = (blk, x * 2 + (1 - c))
    x_side = (blk, (1 - x) * 2 + c)
    y_side = (z * 2 + (1 - y), head)

    def z_side(f):
        return (flip(f) * 2 + y, head)

    barrier = pltpu.get_barrier_semaphore()
    for device in (sibling, x_side, y_side):
        pl.semaphore_signal(barrier, inc=1, device_id=device, device_id_type=MESH)

    @pl.when(zz == 0)
    def _():
        pl.semaphore_signal(barrier, inc=1, device_id=z_side(1), device_id_type=MESH)

    @pl.when(zz == 1)
    def _():
        for f in (0, 2):
            pl.semaphore_signal(barrier, inc=1, device_id=z_side(f), device_id_type=MESH)

    own_q = pltpu.make_async_copy(q_hbm, q_ref, local_sem.at[0])
    own_k = pltpu.make_async_copy(k_hbm, k_buf.at[me], local_sem.at[1])
    own_v = pltpu.make_async_copy(v_hbm, v_buf.at[me], local_sem.at[2])
    own_k.start()
    own_v.start()
    own_q.start()
    pl.semaphore_wait(barrier, 4 + zz)

    K = (k_hbm, k_buf, k_recv, k_send)
    V = (v_hbm, v_buf, v_recv, v_send)
    SIB, XS, YS, ZU, ZD = range(5)

    def copy(which, d, way, device, own=False):
        source, buf, recv, send = which
        return pltpu.make_async_remote_copy(
            src_ref=source if own else buf.at[d], dst_ref=buf.at[d],
            send_sem=send.at[way, d // 2], recv_sem=recv.at[d],
            device_id=device, device_id_type=MESH)

    def arrived(which, d):
        copy(which, d, SIB, sibling).wait_recv()

    def up_down(which, i, d, wait=False):
        def go(way, f):
            one = copy(which, d, way, z_side(f), own=i == 0)
            one.wait_send() if wait else one.start()

        if i == 0:
            @pl.when(zz == 0)
            def _():
                go(ZU, 1)

        @pl.when(zz == 1)
        def _():
            if i == 0:
                go(ZU, 2)
                go(ZD, 0)
            else:
                go(ZU if i == 1 else ZD, 2 if i == 1 else 0)

    def first(i):
        p = plane(i)
        a = shard(p, 0, 0)
        own = i == 0
        if not own:
            arrived(K, a)
        copy(K, a, YS, y_side, own).start()
        up_down(K, i, a)
        if not own:
            arrived(V, a)
        copy(V, a, XS, x_side, own).start()
        up_down(V, i, a)
        copy(K, a, XS, x_side, own).start()
        copy(V, a, YS, y_side, own).start()
        copy(K, a, SIB, sibling, own).start()
        copy(V, a, SIB, sibling, own).start()

    def second(i):
        p = plane(i)
        b, d = shard(p, 1, 0), shard(p, 0, 1)
        arrived(K, b)
        copy(K, b, XS, x_side).start()
        arrived(V, d)
        copy(V, d, YS, y_side).start()
        copy(K, b, SIB, sibling).start()
        copy(V, d, SIB, sibling).start()

    def third(i):
        p = plane(i)
        k_d, v_d = shard(p, 0, 1), shard(p, 1, 0)
        arrived(K, k_d)
        copy(K, k_d, SIB, sibling).start()
        arrived(V, v_d)
        copy(V, v_d, SIB, sibling).start()

    def fourth(i):
        p = plane(i)
        d = shard(p, 1, 1)
        arrived(K, d)
        copy(K, d, SIB, sibling).start()
        arrived(V, d)
        copy(V, d, SIB, sibling).start()

    def from_sibling(i):
        p = plane(i)
        for dy, dx in ((0, 0), (1, 0), (0, 1), (1, 1)):
            arrived(K, shard(p, dy, dx, 1))
            arrived(V, shard(p, dy, dx, 1))

    pos, begin = query_limits(lengths_ref, order_ref, me * rows, rows, block_length)
    slots = 8 * rows // block_length

    def prepare(i):
        fill_bias(bias_ref, order_ref, plane(i) * slots, pos, begin, block_length)

    def compute(i, lo, hi_):
        p = plane(i)

        @pl.loop(lo, hi_)
        def _(g):
            k = k_buf[pl.ds(p * 8, 8), :, head_columns(g)].reshape(8 * rows, HEAD_WIDTH)
            v = v_buf[pl.ds(p * 8, 8), :, head_columns(g)].reshape(8 * rows, HEAD_WIDTH)
            attend(g, k, v, qt_ref, bias_ref, top_ref, total_ref, accum_ref)
            if i == 3:
                finish(g, out_ref, total_ref, accum_ref, rows, ratio)

    first(0)
    reset(top_ref, total_ref, accum_ref)
    own_q.wait()
    pl.loop(0, groups)(lambda g: stack_queries(g, q_ref, qt_ref, ratio))
    second(0)
    first(1)
    third(0)
    fourth(0)
    own_k.wait()
    own_v.wait()
    for i in range(4):
        from_sibling(i)
        prepare(i)
        if i < 3:
            compute(i, 0, 2)
            second(i + 1)
            compute(i, 2, 4)
            if i < 2:
                first(i + 2)
            third(i + 1)
            compute(i, 4, groups)
            fourth(i + 1)
        else:
            compute(i, 0, groups)

    for i in range(4):
        p = plane(i)
        a, b, d, e = shard(p, 0, 0), shard(p, 1, 0), shard(p, 0, 1), shard(p, 1, 1)
        for which, extra in ((K, (b, XS, x_side)), (V, (d, YS, y_side))):
            copy(which, a, XS, x_side).wait_send()
            copy(which, a, YS, y_side).wait_send()
            copy(which, *extra).wait_send()
            up_down(which, i, a, wait=True)
            for s in (a, b, d, e):
                copy(which, s, SIB, sibling).wait_send()


def body(relayed, queries, keys, values, doc_lengths, stored_block_order):
    rows = queries.shape[0]
    groups = keys.shape[1] // HEAD_WIDTH
    ratio = queries.shape[1] // keys.shape[1]
    devices = lax.axis_size("blk") * lax.axis_size("head")
    block_length = rows * devices // stored_block_order.shape[0]
    chunk = max(512, block_length)
    scratch = [
        pltpu.VMEM((groups, HEAD_WIDTH, ratio * rows), BF16),
        pltpu.VMEM((chunk, LANES), F32),
        pltpu.VMEM((groups, 1, ratio * rows), F32),
        pltpu.VMEM((groups, 1, ratio * rows), F32),
        pltpu.VMEM((groups, HEAD_WIDTH, ratio * rows), F32),
    ]
    smem = pl.BlockSpec(memory_space=pltpu.SMEM)
    out_shape = jax.ShapeDtypeStruct(queries.shape, BF16)
    if relayed:
        gathered = pltpu.VMEM((devices, rows, keys.shape[1]), BF16)
        return pl.pallas_call(
            functools.partial(gather_kernel, ratio, block_length),
            out_shape=out_shape,
            in_specs=[smem, smem] + [pl.BlockSpec(memory_space=pl.ANY)] * 3,
            out_specs=pl.BlockSpec(memory_space=pltpu.VMEM),
            scratch_shapes=[pltpu.VMEM(queries.shape, BF16), gathered, gathered] + scratch + [
                pltpu.SemaphoreType.DMA((3,)),
                pltpu.SemaphoreType.DMA((devices,)),
                pltpu.SemaphoreType.DMA((devices,)),
                pltpu.SemaphoreType.DMA((5, devices // 2)),
                pltpu.SemaphoreType.DMA((5, devices // 2)),
            ],
            compiler_params=pltpu.CompilerParams(
                collective_id=0, has_side_effects=True, vmem_limit_bytes=48 << 20),
        )(doc_lengths, stored_block_order, queries, keys, values)
    keys = lax.all_gather(keys, ("blk", "head"), axis=0, tiled=True)
    values = lax.all_gather(values, ("blk", "head"), axis=0, tiled=True)
    first_row = (lax.axis_index("blk") * lax.axis_size("head") + lax.axis_index("head")) * rows
    whole = pl.BlockSpec(queries.shape, lambda i: (0, 0))
    part = pl.BlockSpec((chunk, keys.shape[1]), lambda i: (i, 0))
    return pl.pallas_call(
        functools.partial(chunk_kernel, ratio, block_length),
        out_shape=out_shape,
        grid=(keys.shape[0] // chunk,),
        in_specs=[smem, smem, smem, whole, part, part],
        out_specs=whole,
        scratch_shapes=scratch,
        compiler_params=pltpu.CompilerParams(vmem_limit_bytes=48 << 20),
    )(first_row.reshape(1), doc_lengths, stored_block_order, queries, keys, values)


def solution(mesh):
    rows = P(("blk", "head"), None)
    relayed = mesh.shape["blk"] == 8 and mesh.shape["head"] == 4
    return jax.shard_map(
        functools.partial(body, relayed), mesh=mesh,
        in_specs=(rows, rows, rows, P(), P()), out_specs=rows, check_vma=False)
```

```python
import functools
import math

import jax
import jax.numpy as jnp
from jax import lax
from jax.experimental import pallas as pl
from jax.experimental.pallas import tpu as pltpu
from jax.sharding import PartitionSpec as P

HEAD_WIDTH = 128
LANES = 128
SCORE_TO_LOG2 = HEAD_WIDTH ** (-0.5) * math.log2(math.e)
MASKED = -1e30
START_TOP = -1e25
F32 = jnp.float32
BF16 = jnp.bfloat16
MESH = pl.DeviceIdType.MESH


def query_limits(lengths_ref, order_ref, first_row, rows, block_length):
    lane = lax.broadcasted_iota(jnp.int32, (1, LANES), 1) % rows
    slot = first_row // block_length
    pos = order_ref[slot] * block_length + first_row % block_length + lane
    begin = jnp.zeros_like(pos)
    end = jnp.int32(0)
    for i in range(lengths_ref.shape[0]):
        end = end + lengths_ref[i]
        begin = jnp.where(pos >= end, end, begin)
    return pos, begin


def fill_bias(bias_ref, j, order_ref, slot, pos, begin, block_length):
    key = (
        order_ref[slot] * block_length
        + lax.broadcasted_iota(jnp.int32, (block_length, LANES), 0)
    )
    allowed = (key <= pos) & (key >= begin)
    bias_ref[j * block_length : (j + 1) * block_length, :] = jnp.where(
        allowed, 0.0, MASKED
    ).astype(F32)


def stack_queries(g, q_ref, qt_ref, ratio):
    heads = [
        q_ref[:, pl.ds(pl.multiple_of((g * ratio + j) * HEAD_WIDTH, HEAD_WIDTH), HEAD_WIDTH)]
        for j in range(ratio)
    ]
    qt_ref[g] = jnp.concatenate(heads, axis=0).T


def attend(g, k, v, qt_ref, bias_ref, top_ref, total_ref, accum_ref):
    width = qt_ref.shape[2]
    scores = jnp.dot(k, qt_ref[g], preferred_element_type=F32)
    scores = scores + jnp.concatenate([bias_ref[: k.shape[0]]] * (width // LANES), axis=1)
    top = top_ref[g]
    new_top = jnp.maximum(top, jnp.max(scores, axis=0, keepdims=True))
    weights = jnp.exp2((scores - new_top) * SCORE_TO_LOG2)
    factor = jnp.exp2((top - new_top) * SCORE_TO_LOG2)
    top_ref[g] = new_top
    total_ref[g] = total_ref[g] * factor + jnp.sum(weights, axis=0, keepdims=True)
    accum_ref[g] = accum_ref[g] * factor + jnp.dot(
        v.T, weights.astype(BF16), preferred_element_type=F32
    )


def finish(g, out_ref, total_ref, accum_ref, rows, ratio):
    result = (accum_ref[g] / total_ref[g]).T.astype(BF16)
    for j in range(ratio):
        cols = pl.ds(pl.multiple_of((g * ratio + j) * HEAD_WIDTH, HEAD_WIDTH), HEAD_WIDTH)
        out_ref[:, cols] = result[j * rows : (j + 1) * rows]


def reset(top_ref, total_ref, accum_ref):
    top_ref[...] = jnp.full(top_ref.shape, START_TOP, F32)
    total_ref[...] = jnp.zeros(total_ref.shape, F32)
    accum_ref[...] = jnp.zeros(accum_ref.shape, F32)


def head_columns(g):
    return pl.ds(pl.multiple_of(g * HEAD_WIDTH, HEAD_WIDTH), HEAD_WIDTH)


def chunk_kernel(ratio, block_length, first_ref, lengths_ref, order_ref, q_ref, k_ref, v_ref,
                 out_ref, qt_ref, bias_ref, top_ref, total_ref, accum_ref):
    step = pl.program_id(0)
    rows = q_ref.shape[0]
    groups = k_ref.shape[1] // HEAD_WIDTH
    chunk = k_ref.shape[0]

    @pl.when(step == 0)
    def _():
        reset(top_ref, total_ref, accum_ref)
        pl.loop(0, groups)(lambda g: stack_queries(g, q_ref, qt_ref, ratio))

    pos, begin = query_limits(lengths_ref, order_ref, first_ref[0], rows, block_length)
    slots = chunk // block_length
    for j in range(slots):
        fill_bias(bias_ref, j, order_ref, step * slots + j, pos, begin, block_length)

    @pl.loop(0, groups)
    def _(g):
        attend(g, k_ref[:, head_columns(g)], v_ref[:, head_columns(g)],
               qt_ref, bias_ref, top_ref, total_ref, accum_ref)

    @pl.when(step == pl.num_programs(0) - 1)
    def _():
        pl.loop(0, groups)(lambda g: finish(g, out_ref, total_ref, accum_ref, rows, ratio))


def gather_kernel(ratio, block_length, lengths_hbm, order_hbm, q_hbm, k_hbm, v_hbm, out_ref,
                  lengths_ref, order_ref, q_ref, k_buf, v_buf, qt_ref, bias_ref, top_ref, total_ref, accum_ref,
                  local_sem, k_recv, v_recv, k_send, v_send):
    rows, width = k_hbm.shape
    groups = width // HEAD_WIDTH
    blk, head = lax.axis_index("blk"), lax.axis_index("head")
    z, y, x, c = blk // 2, blk % 2, head // 2, head % 2
    me = blk * 4 + head
    hi = z // 2
    zz = z + hi * (3 - 2 * z)

    def flip(f):
        return f + hi * (3 - 2 * f)

    def plane(i):
        return flip(i + zz * (1 - 2 * i)) if i < 2 else flip(i)

    def shard(p, dy, dx, dc=0):
        yy = y + dy * (1 - 2 * y)
        xx = x + dx * (1 - 2 * x)
        cc = c + dc * (1 - 2 * c)
        return ((p * 2 + yy) * 2 + xx) * 2 + cc

    sibling = (blk, x * 2 + (1 - c))
    x_side = (blk, (1 - x) * 2 + c)
    y_side = (z * 2 + (1 - y), head)

    def z_side(f):
        return (flip(f) * 2 + y, head)

    barrier = pltpu.get_barrier_semaphore()
    for device in (sibling, x_side, y_side):
        pl.semaphore_signal(barrier, inc=1, device_id=device, device_id_type=MESH)

    @pl.when(zz == 0)
    def _():
        pl.semaphore_signal(barrier, inc=1, device_id=z_side(1), device_id_type=MESH)

    @pl.when(zz == 1)
    def _():
        for f in (0, 2):
            pl.semaphore_signal(barrier, inc=1, device_id=z_side(f), device_id_type=MESH)

    own_q = pltpu.make_async_copy(q_hbm, q_ref, local_sem.at[0])
    own_k = pltpu.make_async_copy(k_hbm, k_buf.at[me], local_sem.at[1])
    own_v = pltpu.make_async_copy(v_hbm, v_buf.at[me], local_sem.at[2])
    own_k.start()
    own_v.start()
    own_q.start()
    own_lengths = pltpu.make_async_copy(lengths_hbm, lengths_ref, local_sem.at[3])
    own_order = pltpu.make_async_copy(order_hbm, order_ref, local_sem.at[4])
    own_lengths.start()
    own_order.start()
    pl.semaphore_wait(barrier, 4 + zz)

    K = (k_hbm, k_buf, k_recv, k_send)
    V = (v_hbm, v_buf, v_recv, v_send)
    SIB, XS, YS, ZU, ZD = range(5)

    def copy(which, d, way, device, own=False):
        source, buf, recv, send = which
        return pltpu.make_async_remote_copy(
            src_ref=source if own else buf.at[d], dst_ref=buf.at[d],
            send_sem=send.at[way, d // 2], recv_sem=recv.at[d],
            device_id=device, device_id_type=MESH)

    def arrived(which, d):
        copy(which, d, SIB, sibling).wait_recv()

    def up_down(which, i, d, wait=False, own=False):
        def go(way, f):
            one = copy(which, d, way, z_side(f), own=own)
            one.wait_send() if wait else one.start()

        if i == 0:
            @pl.when(zz == 0)
            def _():
                go(ZU, 1)

        @pl.when(zz == 1)
        def _():
            if i == 0:
                go(ZU, 2)
                go(ZD, 0)
            else:
                go(ZU if i == 1 else ZD, 2 if i == 1 else 0)

    def relay(i, dy, dx):
        @pl.when(zz == 1)
        def _():
            d = shard(plane(i), dy, dx)
            for which in (K, V):
                arrived(which, d)
                copy(which, d, ZD, z_side(0)).start()

    def arrived_unless_relayed(which, d):
        @pl.when(zz == 0)
        def _():
            arrived(which, d)

    def first(i):
        a = shard(plane(i), 0, 0)
        own = i == 0
        meet = arrived if i == 1 else arrived_unless_relayed
        if not own:
            meet(K, a)
        copy(K, a, YS, y_side, own).start()
        if i < 2:
            up_down(K, i, a, own=own)
        if not own:
            meet(V, a)
        copy(V, a, XS, x_side, own).start()
        if i < 2:
            up_down(V, i, a, own=own)
        copy(K, a, XS, x_side, own).start()
        copy(V, a, YS, y_side, own).start()
        copy(K, a, SIB, sibling, own).start()
        copy(V, a, SIB, sibling, own).start()

    def second(i):
        p = plane(i)
        b, d = shard(p, 1, 0), shard(p, 0, 1)
        arrived(K, b)
        if i in (0, 3):
            copy(K, b, XS, x_side).start()
        arrived(V, d)
        if i in (0, 3):
            copy(V, d, YS, y_side).start()
        copy(K, b, SIB, sibling).start()
        copy(V, d, SIB, sibling).start()

    def third(i):
        p = plane(i)
        k_d, v_d = shard(p, 0, 1), shard(p, 1, 0)
        arrived(K, k_d)
        copy(K, k_d, SIB, sibling).start()
        arrived(V, v_d)
        copy(V, v_d, SIB, sibling).start()

    def fourth(i):
        d = shard(plane(i), 1, 1)
        for which in (K, V):
            (arrived_unless_relayed if i == 2 else arrived)(which, d)
            if i == 0:
                up_down(which, i, d)
        for which in (K, V):
            copy(which, d, SIB, sibling).start()

    def from_sibling(chunk):
        for i, dy, dx in chunk:
            arrived(K, shard(plane(i), dy, dx, 1))
            arrived(V, shard(plane(i), dy, dx, 1))

    def prepare(chunk):
        for j, (i, dy, dx) in enumerate(chunk):
            fill_bias(bias_ref, j, order_ref, shard(plane(i), dy, dx) // 2, pos, begin,
                      block_length)

    def compute(chunk, lo, hi_, last=False):
        pairs = [shard(plane(i), dy, dx) // 2 * 2 for i, dy, dx in chunk]

        @pl.loop(lo, hi_)
        def _(g):
            k, v = (
                jnp.concatenate([
                    buf[pl.ds(d, 2), :, head_columns(g)].reshape(2 * rows, HEAD_WIDTH)
                    for d in pairs
                ], axis=0)
                for buf in (k_buf, v_buf)
            )
            attend(g, k, v, qt_ref, bias_ref, top_ref, total_ref, accum_ref)
            if last:
                finish(g, out_ref, total_ref, accum_ref, rows, ratio)

    def near(i):
        return [(i, 0, 0), (i, 1, 0), (i, 0, 1)]

    def far(i):
        return [(i, 1, 1)]

    first(0)
    own_lengths.wait()
    own_order.wait()
    pos, begin = query_limits(lengths_ref, order_ref, me * rows, rows, block_length)
    reset(top_ref, total_ref, accum_ref)
    own_q.wait()
    pl.loop(0, groups)(lambda g: stack_queries(g, q_ref, qt_ref, ratio))
    second(0)
    first(1)
    relay(2, 0, 0)
    third(0)
    fourth(0)
    own_k.wait()
    own_v.wait()
    go = functools.partial
    steps = [
        (near(0) + far(0), [go(second, 1), go(first, 2), go(relay, 3, 0, 0), go(third, 1)]),
        (near(1), [go(second, 2), go(first, 3), go(relay, 2, 1, 1), go(third, 2)]),
        (near(2), [go(second, 3), go(fourth, 1), go(third, 3)]),
        (near(3) + far(1), [go(fourth, 2), go(fourth, 3)]),
        (far(2) + far(3), []),
    ]
    for n, (chunk, events) in enumerate(steps):
        from_sibling(chunk)
        prepare(chunk)
        done = 0
        for event in events:
            compute(chunk, done, done + 2)
            done += 2
            event()
        if done < groups:
            compute(chunk, done, groups, last=n == len(steps) - 1)

    for i in range(4):
        p = plane(i)
        a, b, d, e = shard(p, 0, 0), shard(p, 1, 0), shard(p, 0, 1), shard(p, 1, 1)
        for which, extra in ((K, (b, XS, x_side)), (V, (d, YS, y_side))):
            copy(which, a, XS, x_side).wait_send()
            copy(which, a, YS, y_side).wait_send()
            if i in (0, 3):
                copy(which, *extra).wait_send()
            up_down(which, i, a, wait=True)
            if i in (0, 2):
                up_down(which, i, e, wait=True)
            for s in (a, b, d, e):
                copy(which, s, SIB, sibling).wait_send()


def body(relayed, queries, keys, values, doc_lengths, stored_block_order):
    rows = queries.shape[0]
    groups = keys.shape[1] // HEAD_WIDTH
    ratio = queries.shape[1] // keys.shape[1]
    devices = lax.axis_size("blk") * lax.axis_size("head")
    block_length = rows * devices // stored_block_order.shape[0]
    chunk = max(512, block_length)
    scratch = [
        pltpu.VMEM((groups, HEAD_WIDTH, ratio * rows), BF16),
        pltpu.VMEM((chunk, LANES), F32),
        pltpu.VMEM((groups, 1, ratio * rows), F32),
        pltpu.VMEM((groups, 1, ratio * rows), F32),
        pltpu.VMEM((groups, HEAD_WIDTH, ratio * rows), F32),
    ]
    smem = pl.BlockSpec(memory_space=pltpu.SMEM)
    out_shape = jax.ShapeDtypeStruct(queries.shape, BF16)
    if relayed:
        gathered = pltpu.VMEM((devices, rows, keys.shape[1]), BF16)
        return pl.pallas_call(
            functools.partial(gather_kernel, ratio, block_length),
            out_shape=out_shape,
            in_specs=[pl.BlockSpec(memory_space=pltpu.HBM)] * 5,
            out_specs=pl.BlockSpec(memory_space=pltpu.VMEM),
            scratch_shapes=[pltpu.SMEM(doc_lengths.shape, jnp.int32),
                            pltpu.SMEM(stored_block_order.shape, jnp.int32),
                            pltpu.VMEM(queries.shape, BF16), gathered, gathered] + scratch + [
                pltpu.SemaphoreType.DMA((5,)),
                pltpu.SemaphoreType.DMA((devices,)),
                pltpu.SemaphoreType.DMA((devices,)),
                pltpu.SemaphoreType.DMA((5, devices // 2)),
                pltpu.SemaphoreType.DMA((5, devices // 2)),
            ],
            compiler_params=pltpu.CompilerParams(
                collective_id=0, has_side_effects=True, vmem_limit_bytes=48 << 20),
        )(doc_lengths, stored_block_order, queries, keys, values)
    keys = lax.all_gather(keys, ("blk", "head"), axis=0, tiled=True)
    values = lax.all_gather(values, ("blk", "head"), axis=0, tiled=True)
    first_row = (lax.axis_index("blk") * lax.axis_size("head") + lax.axis_index("head")) * rows
    whole = pl.BlockSpec(queries.shape, lambda i: (0, 0))
    part = pl.BlockSpec((chunk, keys.shape[1]), lambda i: (i, 0))
    return pl.pallas_call(
        functools.partial(chunk_kernel, ratio, block_length),
        out_shape=out_shape,
        grid=(keys.shape[0] // chunk,),
        in_specs=[smem, smem, smem, whole, part, part],
        out_specs=whole,
        scratch_shapes=scratch,
        compiler_params=pltpu.CompilerParams(vmem_limit_bytes=48 << 20),
    )(first_row.reshape(1), doc_lengths, stored_block_order, queries, keys, values)


def solution(mesh):
    rows = P(("blk", "head"), None)
    relayed = mesh.shape["blk"] == 8 and mesh.shape["head"] == 4
    return jax.shard_map(
        functools.partial(body, relayed), mesh=mesh,
        in_specs=(rows, rows, rows, P(), P()), out_specs=rows, check_vma=False)
```

```python
import functools
import math

import jax
import jax.numpy as jnp
from jax import lax
from jax.experimental import pallas as pl
from jax.experimental.pallas import tpu as pltpu
from jax.sharding import PartitionSpec as P

HEAD_WIDTH = 128
LANES = 128
SCORE_TO_LOG2 = HEAD_WIDTH ** (-0.5) * math.log2(math.e)
MASKED = -1e30
START_TOP = -1e25
F32 = jnp.float32
BF16 = jnp.bfloat16
MESH = pl.DeviceIdType.MESH


def query_limits(lengths_ref, order_ref, first_row, rows, block_length):
    lane = lax.broadcasted_iota(jnp.int32, (1, LANES), 1) % rows
    slot = first_row // block_length
    pos = order_ref[slot] * block_length + first_row % block_length + lane
    begin = jnp.zeros_like(pos)
    end = jnp.int32(0)
    for i in range(lengths_ref.shape[0]):
        end = end + lengths_ref[i]
        begin = jnp.where(pos >= end, end, begin)
    return pos, begin


def fill_bias(bias_ref, j, order_ref, slot, pos, begin, block_length):
    key = (
        order_ref[slot] * block_length
        + lax.broadcasted_iota(jnp.int32, (block_length, LANES), 0)
    )
    allowed = (key <= pos) & (key >= begin)
    bias_ref[j * block_length : (j + 1) * block_length, :] = jnp.where(
        allowed, 0.0, MASKED
    ).astype(F32)


def stack_queries(g, q_ref, qt_ref, ratio):
    heads = [
        q_ref[:, pl.ds(pl.multiple_of((g * ratio + j) * HEAD_WIDTH, HEAD_WIDTH), HEAD_WIDTH)]
        for j in range(ratio)
    ]
    qt_ref[g] = jnp.concatenate(heads, axis=0).T


def attend(gs, ks, vs, qt_ref, bias_ref, top_ref, total_ref, accum_ref):
    width = qt_ref.shape[2]
    bias = jnp.concatenate([bias_ref[: ks[0].shape[0]]] * (width // LANES), axis=1)
    states = [(top_ref[g], total_ref[g], accum_ref[g]) for g in gs]
    scores = [jnp.dot(k, qt_ref[g], preferred_element_type=F32) for g, k in zip(gs, ks)]
    results = []
    for (top, total, accum), s, v in zip(states, scores, vs):
        s = s + bias
        new_top = jnp.maximum(top, jnp.max(s, axis=0, keepdims=True))
        weights = jnp.exp2((s - new_top) * SCORE_TO_LOG2)
        factor = jnp.exp2((top - new_top) * SCORE_TO_LOG2)
        total = total * factor + jnp.sum(weights, axis=0, keepdims=True)
        accum = accum * factor + jnp.dot(
            v.T, weights.astype(BF16), preferred_element_type=F32
        )
        results.append((new_top, total, accum))
    for g, (top, total, accum) in zip(gs, results):
        top_ref[g] = top
        total_ref[g] = total
        accum_ref[g] = accum


def finish(g, out_ref, total_ref, accum_ref, rows, ratio):
    result = (accum_ref[g] / total_ref[g]).T.astype(BF16)
    for j in range(ratio):
        cols = pl.ds(pl.multiple_of((g * ratio + j) * HEAD_WIDTH, HEAD_WIDTH), HEAD_WIDTH)
        out_ref[:, cols] = result[j * rows : (j + 1) * rows]


def reset(top_ref, total_ref, accum_ref):
    top_ref[...] = jnp.full(top_ref.shape, START_TOP, F32)
    total_ref[...] = jnp.zeros(total_ref.shape, F32)
    accum_ref[...] = jnp.zeros(accum_ref.shape, F32)


def head_columns(g):
    return pl.ds(pl.multiple_of(g * HEAD_WIDTH, HEAD_WIDTH), HEAD_WIDTH)


def chunk_kernel(ratio, block_length, first_ref, lengths_ref, order_ref, q_ref, k_ref, v_ref,
                 out_ref, qt_ref, bias_ref, top_ref, total_ref, accum_ref):
    step = pl.program_id(0)
    rows = q_ref.shape[0]
    groups = k_ref.shape[1] // HEAD_WIDTH
    chunk = k_ref.shape[0]

    @pl.when(step == 0)
    def _():
        reset(top_ref, total_ref, accum_ref)
        pl.loop(0, groups)(lambda g: stack_queries(g, q_ref, qt_ref, ratio))

    pos, begin = query_limits(lengths_ref, order_ref, first_ref[0], rows, block_length)
    slots = chunk // block_length
    for j in range(slots):
        fill_bias(bias_ref, j, order_ref, step * slots + j, pos, begin, block_length)

    @pl.loop(0, groups)
    def _(g):
        attend([g], [k_ref[:, head_columns(g)]], [v_ref[:, head_columns(g)]],
               qt_ref, bias_ref, top_ref, total_ref, accum_ref)

    @pl.when(step == pl.num_programs(0) - 1)
    def _():
        pl.loop(0, groups)(lambda g: finish(g, out_ref, total_ref, accum_ref, rows, ratio))


def gather_kernel(ratio, block_length, lengths_hbm, order_hbm, q_hbm, k_hbm, v_hbm, out_ref,
                  lengths_ref, order_ref, q_ref, k_buf, v_buf, qt_ref, bias_ref, top_ref, total_ref, accum_ref,
                  local_sem, k_recv, v_recv, k_send, v_send):
    rows, width = k_hbm.shape
    groups = width // HEAD_WIDTH
    blk, head = lax.axis_index("blk"), lax.axis_index("head")
    z, y, x, c = blk // 2, blk % 2, head // 2, head % 2
    me = blk * 4 + head
    hi = z // 2
    zz = z + hi * (3 - 2 * z)

    def flip(f):
        return f + hi * (3 - 2 * f)

    def plane(i):
        return flip(i + zz * (1 - 2 * i)) if i < 2 else flip(i)

    def shard(p, dy, dx, dc=0):
        yy = y + dy * (1 - 2 * y)
        xx = x + dx * (1 - 2 * x)
        cc = c + dc * (1 - 2 * c)
        return ((p * 2 + yy) * 2 + xx) * 2 + cc

    sibling = (blk, x * 2 + (1 - c))
    x_side = (blk, (1 - x) * 2 + c)
    y_side = (z * 2 + (1 - y), head)

    def z_side(f):
        return (flip(f) * 2 + y, head)

    barrier = pltpu.get_barrier_semaphore()
    for device in (sibling, x_side, y_side):
        pl.semaphore_signal(barrier, inc=1, device_id=device, device_id_type=MESH)

    @pl.when(zz == 0)
    def _():
        pl.semaphore_signal(barrier, inc=1, device_id=z_side(1), device_id_type=MESH)

    @pl.when(zz == 1)
    def _():
        for f in (0, 2):
            pl.semaphore_signal(barrier, inc=1, device_id=z_side(f), device_id_type=MESH)

    own_q = pltpu.make_async_copy(q_hbm, q_ref, local_sem.at[0])
    own_k = pltpu.make_async_copy(k_hbm, k_buf.at[me], local_sem.at[1])
    own_v = pltpu.make_async_copy(v_hbm, v_buf.at[me], local_sem.at[2])
    own_k.start()
    own_v.start()
    own_q.start()
    own_lengths = pltpu.make_async_copy(lengths_hbm, lengths_ref, local_sem.at[3])
    own_order = pltpu.make_async_copy(order_hbm, order_ref, local_sem.at[4])
    own_lengths.start()
    own_order.start()
    pl.semaphore_wait(barrier, 4 + zz)

    K = (k_hbm, k_buf, k_recv, k_send)
    V = (v_hbm, v_buf, v_recv, v_send)
    SIB, XS, YS, ZU, ZD = range(5)

    def copy(which, d, way, device, own=False):
        source, buf, recv, send = which
        return pltpu.make_async_remote_copy(
            src_ref=source if own else buf.at[d], dst_ref=buf.at[d],
            send_sem=send.at[way, d // 2], recv_sem=recv.at[d],
            device_id=device, device_id_type=MESH)

    def arrived(which, d):
        copy(which, d, SIB, sibling).wait_recv()

    def up_down(which, i, d, wait=False, own=False):
        def go(way, f):
            one = copy(which, d, way, z_side(f), own=own)
            one.wait_send() if wait else one.start()

        if i == 0:
            @pl.when(zz == 0)
            def _():
                go(ZU, 1)

        @pl.when(zz == 1)
        def _():
            if i == 0:
                go(ZU, 2)
                go(ZD, 0)
            else:
                go(ZU if i == 1 else ZD, 2 if i == 1 else 0)

    def relay(i, dy, dx):
        @pl.when(zz == 1)
        def _():
            d = shard(plane(i), dy, dx)
            for which in (K, V):
                arrived(which, d)
                copy(which, d, ZD, z_side(0)).start()

    def arrived_unless_relayed(which, d):
        @pl.when(zz == 0)
        def _():
            arrived(which, d)

    def first(i):
        a = shard(plane(i), 0, 0)
        own = i == 0
        meet = arrived if i == 1 else arrived_unless_relayed
        if not own:
            meet(K, a)
        copy(K, a, YS, y_side, own).start()
        if i < 2:
            up_down(K, i, a, own=own)
        if not own:
            meet(V, a)
        copy(V, a, XS, x_side, own).start()
        if i < 2:
            up_down(V, i, a, own=own)
        copy(K, a, XS, x_side, own).start()
        copy(V, a, YS, y_side, own).start()
        copy(K, a, SIB, sibling, own).start()
        copy(V, a, SIB, sibling, own).start()

    def second(i):
        p = plane(i)
        b, d = shard(p, 1, 0), shard(p, 0, 1)
        arrived(K, b)
        if i in (0, 3):
            copy(K, b, XS, x_side).start()
        arrived(V, d)
        if i in (0, 3):
            copy(V, d, YS, y_side).start()
        copy(K, b, SIB, sibling).start()
        copy(V, d, SIB, sibling).start()

    def third(i):
        p = plane(i)
        k_d, v_d = shard(p, 0, 1), shard(p, 1, 0)
        arrived(K, k_d)
        copy(K, k_d, SIB, sibling).start()
        arrived(V, v_d)
        copy(V, v_d, SIB, sibling).start()

    def fourth(i):
        d = shard(plane(i), 1, 1)
        for which in (K, V):
            (arrived_unless_relayed if i == 2 else arrived)(which, d)
            if i == 0:
                up_down(which, i, d)
        for which in (K, V):
            copy(which, d, SIB, sibling).start()

    def from_sibling(chunk):
        for i, dy, dx in chunk:
            arrived(K, shard(plane(i), dy, dx, 1))
            arrived(V, shard(plane(i), dy, dx, 1))

    def prepare(chunk):
        for j, (i, dy, dx) in enumerate(chunk):
            fill_bias(bias_ref, j, order_ref, shard(plane(i), dy, dx) // 2, pos, begin,
                      block_length)

    def compute(chunk, lo, hi_, last=False):
        pairs = [shard(plane(i), dy, dx) // 2 * 2 for i, dy, dx in chunk]

        def load(buf, g):
            return jnp.concatenate([
                buf[pl.ds(d, 2), :, head_columns(g)].reshape(2 * rows, HEAD_WIDTH)
                for d in pairs
            ], axis=0)

        @pl.loop(lo, hi_, step=2)
        def _(first_g):
            gs = [first_g + j for j in range(2)]
            attend(gs, [load(k_buf, g) for g in gs], [load(v_buf, g) for g in gs],
                   qt_ref, bias_ref, top_ref, total_ref, accum_ref)
            if last:
                for g in gs:
                    finish(g, out_ref, total_ref, accum_ref, rows, ratio)

    def near(i):
        return [(i, 0, 0), (i, 1, 0), (i, 0, 1)]

    def far(i):
        return [(i, 1, 1)]

    first(0)
    own_lengths.wait()
    own_order.wait()
    pos, begin = query_limits(lengths_ref, order_ref, me * rows, rows, block_length)
    reset(top_ref, total_ref, accum_ref)
    own_q.wait()
    pl.loop(0, groups)(lambda g: stack_queries(g, q_ref, qt_ref, ratio))
    second(0)
    first(1)
    relay(2, 0, 0)
    third(0)
    fourth(0)
    own_k.wait()
    own_v.wait()
    go = functools.partial
    steps = [
        (near(0) + far(0), [go(second, 1), go(first, 2), go(relay, 3, 0, 0), go(third, 1)]),
        (near(1), [go(second, 2), go(first, 3), go(relay, 2, 1, 1), go(third, 2)]),
        (near(2), [go(second, 3), go(fourth, 1), go(third, 3)]),
        (near(3) + far(1), [go(fourth, 2), go(fourth, 3)]),
        (far(2) + far(3), []),
    ]
    for n, (chunk, events) in enumerate(steps):
        from_sibling(chunk)
        prepare(chunk)
        done = 0
        for event in events:
            compute(chunk, done, done + 2)
            done += 2
            event()
        if done < groups:
            compute(chunk, done, groups, last=n == len(steps) - 1)

    for i in range(4):
        p = plane(i)
        a, b, d, e = shard(p, 0, 0), shard(p, 1, 0), shard(p, 0, 1), shard(p, 1, 1)
        for which, extra in ((K, (b, XS, x_side)), (V, (d, YS, y_side))):
            copy(which, a, XS, x_side).wait_send()
            copy(which, a, YS, y_side).wait_send()
            if i in (0, 3):
                copy(which, *extra).wait_send()
            up_down(which, i, a, wait=True)
            if i in (0, 2):
                up_down(which, i, e, wait=True)
            for s in (a, b, d, e):
                copy(which, s, SIB, sibling).wait_send()


def body(relayed, queries, keys, values, doc_lengths, stored_block_order):
    rows = queries.shape[0]
    groups = keys.shape[1] // HEAD_WIDTH
    ratio = queries.shape[1] // keys.shape[1]
    devices = lax.axis_size("blk") * lax.axis_size("head")
    block_length = rows * devices // stored_block_order.shape[0]
    chunk = max(512, block_length)
    scratch = [
        pltpu.VMEM((groups, HEAD_WIDTH, ratio * rows), BF16),
        pltpu.VMEM((chunk, LANES), F32),
        pltpu.VMEM((groups, 1, ratio * rows), F32),
        pltpu.VMEM((groups, 1, ratio * rows), F32),
        pltpu.VMEM((groups, HEAD_WIDTH, ratio * rows), F32),
    ]
    smem = pl.BlockSpec(memory_space=pltpu.SMEM)
    out_shape = jax.ShapeDtypeStruct(queries.shape, BF16)
    if relayed:
        gathered = pltpu.VMEM((devices, rows, keys.shape[1]), BF16)
        return pl.pallas_call(
            functools.partial(gather_kernel, ratio, block_length),
            out_shape=out_shape,
            in_specs=[pl.BlockSpec(memory_space=pltpu.HBM)] * 5,
            out_specs=pl.BlockSpec(memory_space=pltpu.VMEM),
            scratch_shapes=[pltpu.SMEM(doc_lengths.shape, jnp.int32),
                            pltpu.SMEM(stored_block_order.shape, jnp.int32),
                            pltpu.VMEM(queries.shape, BF16), gathered, gathered] + scratch + [
                pltpu.SemaphoreType.DMA((5,)),
                pltpu.SemaphoreType.DMA((devices,)),
                pltpu.SemaphoreType.DMA((devices,)),
                pltpu.SemaphoreType.DMA((5, devices // 2)),
                pltpu.SemaphoreType.DMA((5, devices // 2)),
            ],
            compiler_params=pltpu.CompilerParams(
                collective_id=0, has_side_effects=True, vmem_limit_bytes=48 << 20),
        )(doc_lengths, stored_block_order, queries, keys, values)
    keys = lax.all_gather(keys, ("blk", "head"), axis=0, tiled=True)
    values = lax.all_gather(values, ("blk", "head"), axis=0, tiled=True)
    first_row = (lax.axis_index("blk") * lax.axis_size("head") + lax.axis_index("head")) * rows
    whole = pl.BlockSpec(queries.shape, lambda i: (0, 0))
    part = pl.BlockSpec((chunk, keys.shape[1]), lambda i: (i, 0))
    return pl.pallas_call(
        functools.partial(chunk_kernel, ratio, block_length),
        out_shape=out_shape,
        grid=(keys.shape[0] // chunk,),
        in_specs=[smem, smem, smem, whole, part, part],
        out_specs=whole,
        scratch_shapes=scratch,
        compiler_params=pltpu.CompilerParams(vmem_limit_bytes=48 << 20),
    )(first_row.reshape(1), doc_lengths, stored_block_order, queries, keys, values)


def solution(mesh):
    rows = P(("blk", "head"), None)
    relayed = mesh.shape["blk"] == 8 and mesh.shape["head"] == 4
    return jax.shard_map(
        functools.partial(body, relayed), mesh=mesh,
        in_specs=(rows, rows, rows, P(), P()), out_specs=rows, check_vma=False)
```

```python
import functools
import math

import jax
import jax.numpy as jnp
from jax import lax
from jax.experimental import pallas as pl
from jax.experimental.pallas import tpu as pltpu
from jax.sharding import PartitionSpec as P

HEAD_WIDTH = 128
LANES = 128
SCORE_TO_LOG2 = HEAD_WIDTH ** (-0.5) * math.log2(math.e)
MASKED = -1e30
START_TOP = -1e25
F32 = jnp.float32
BF16 = jnp.bfloat16
MESH = pl.DeviceIdType.MESH


def query_limits(lengths_ref, order_ref, first_row, rows, block_length):
    lane = lax.broadcasted_iota(jnp.int32, (1, LANES), 1) % rows
    slot = first_row // block_length
    pos = order_ref[slot] * block_length + first_row % block_length + lane
    begin = jnp.zeros_like(pos)
    end = jnp.int32(0)
    for i in range(lengths_ref.shape[0]):
        end = end + lengths_ref[i]
        begin = jnp.where(pos >= end, end, begin)
    return pos, begin


def fill_bias(bias_ref, j, order_ref, slot, pos, begin, block_length):
    key = (
        order_ref[slot] * block_length
        + lax.broadcasted_iota(jnp.int32, (block_length, LANES), 0)
    )
    allowed = (key <= pos) & (key >= begin)
    bias_ref[j * block_length : (j + 1) * block_length, :] = jnp.where(
        allowed, 0.0, MASKED
    ).astype(F32)


def stack_queries(g, q_ref, qt_ref, ratio):
    heads = [
        q_ref[:, pl.ds(pl.multiple_of((g * ratio + j) * HEAD_WIDTH, HEAD_WIDTH), HEAD_WIDTH)]
        for j in range(ratio)
    ]
    qt_ref[g] = jnp.concatenate(heads, axis=0).T


def attend(gs, ks, vs, qt_ref, bias_ref, top_ref, total_ref, accum_ref):
    width = qt_ref.shape[2]
    bias = jnp.concatenate([bias_ref[: ks[0].shape[0]]] * (width // LANES), axis=1)
    states = [(top_ref[g], total_ref[g], accum_ref[g]) for g in gs]
    scores = [jnp.dot(k, qt_ref[g], preferred_element_type=F32) for g, k in zip(gs, ks)]
    results = []
    for (top, total, accum), s, v in zip(states, scores, vs):
        s = s + bias
        new_top = jnp.maximum(top, jnp.max(s, axis=0, keepdims=True))
        weights = jnp.exp2((s - new_top) * SCORE_TO_LOG2)
        factor = jnp.exp2((top - new_top) * SCORE_TO_LOG2)
        both = jnp.dot(jnp.concatenate([v.T, jnp.ones((16, v.shape[0]), BF16)], axis=0), weights.astype(BF16), preferred_element_type=F32)
        accum = accum * factor + both[:HEAD_WIDTH]
        total = total * factor + both[HEAD_WIDTH:HEAD_WIDTH + 1]
        results.append((new_top, total, accum))
    for g, (top, total, accum) in zip(gs, results):
        top_ref[g] = top
        total_ref[g] = total
        accum_ref[g] = accum


def finish(g, out_ref, total_ref, accum_ref, rows, ratio):
    result = (accum_ref[g] / total_ref[g]).T.astype(BF16)
    for j in range(ratio):
        cols = pl.ds(pl.multiple_of((g * ratio + j) * HEAD_WIDTH, HEAD_WIDTH), HEAD_WIDTH)
        out_ref[:, cols] = result[j * rows : (j + 1) * rows]


def reset(top_ref, total_ref, accum_ref):
    top_ref[...] = jnp.full(top_ref.shape, START_TOP, F32)
    total_ref[...] = jnp.zeros(total_ref.shape, F32)
    accum_ref[...] = jnp.zeros(accum_ref.shape, F32)


def head_columns(g):
    return pl.ds(pl.multiple_of(g * HEAD_WIDTH, HEAD_WIDTH), HEAD_WIDTH)


def chunk_kernel(ratio, block_length, first_ref, lengths_ref, order_ref, q_ref, k_ref, v_ref,
                 out_ref, qt_ref, bias_ref, top_ref, total_ref, accum_ref):
    step = pl.program_id(0)
    rows = q_ref.shape[0]
    groups = k_ref.shape[1] // HEAD_WIDTH
    chunk = k_ref.shape[0]

    @pl.when(step == 0)
    def _():
        reset(top_ref, total_ref, accum_ref)
        pl.loop(0, groups)(lambda g: stack_queries(g, q_ref, qt_ref, ratio))

    pos, begin = query_limits(lengths_ref, order_ref, first_ref[0], rows, block_length)
    slots = chunk // block_length
    for j in range(slots):
        fill_bias(bias_ref, j, order_ref, step * slots + j, pos, begin, block_length)

    @pl.loop(0, groups)
    def _(g):
        attend([g], [k_ref[:, head_columns(g)]], [v_ref[:, head_columns(g)]],
               qt_ref, bias_ref, top_ref, total_ref, accum_ref)

    @pl.when(step == pl.num_programs(0) - 1)
    def _():
        pl.loop(0, groups)(lambda g: finish(g, out_ref, total_ref, accum_ref, rows, ratio))


def gather_kernel(ratio, block_length, lengths_hbm, order_hbm, q_hbm, k_hbm, v_hbm, out_ref,
                  lengths_ref, order_ref, q_ref, k_buf, v_buf, qt_ref, bias_ref, top_ref, total_ref, accum_ref,
                  local_sem, k_recv, v_recv, k_send, v_send):
    rows, width = k_hbm.shape
    groups = width // HEAD_WIDTH
    blk, head = lax.axis_index("blk"), lax.axis_index("head")
    z, y, x, c = blk // 2, blk % 2, head // 2, head % 2
    me = blk * 4 + head
    hi = z // 2
    zz = z + hi * (3 - 2 * z)

    def flip(f):
        return f + hi * (3 - 2 * f)

    def plane(i):
        return flip(i + zz * (1 - 2 * i)) if i < 2 else flip(i)

    def shard(p, dy, dx, dc=0):
        yy = y + dy * (1 - 2 * y)
        xx = x + dx * (1 - 2 * x)
        cc = c + dc * (1 - 2 * c)
        return ((p * 2 + yy) * 2 + xx) * 2 + cc

    sibling = (blk, x * 2 + (1 - c))
    x_side = (blk, (1 - x) * 2 + c)
    y_side = (z * 2 + (1 - y), head)

    def z_side(f):
        return (flip(f) * 2 + y, head)

    barrier = pltpu.get_barrier_semaphore()
    for device in (sibling, x_side, y_side):
        pl.semaphore_signal(barrier, inc=1, device_id=device, device_id_type=MESH)

    @pl.when(zz == 0)
    def _():
        pl.semaphore_signal(barrier, inc=1, device_id=z_side(1), device_id_type=MESH)

    @pl.when(zz == 1)
    def _():
        for f in (0, 2):
            pl.semaphore_signal(barrier, inc=1, device_id=z_side(f), device_id_type=MESH)

    own_q = pltpu.make_async_copy(q_hbm, q_ref, local_sem.at[0])
    own_k = pltpu.make_async_copy(k_hbm, k_buf.at[me], local_sem.at[1])
    own_v = pltpu.make_async_copy(v_hbm, v_buf.at[me], local_sem.at[2])
    own_k.start()
    own_v.start()
    own_q.start()
    own_lengths = pltpu.make_async_copy(lengths_hbm, lengths_ref, local_sem.at[3])
    own_order = pltpu.make_async_copy(order_hbm, order_ref, local_sem.at[4])
    own_lengths.start()
    own_order.start()
    pl.semaphore_wait(barrier, 4 + zz)

    K = (k_hbm, k_buf, k_recv, k_send)
    V = (v_hbm, v_buf, v_recv, v_send)
    SIB, XS, YS, ZU, ZD = range(5)

    def copy(which, d, way, device, own=False):
        source, buf, recv, send = which
        return pltpu.make_async_remote_copy(
            src_ref=source if own else buf.at[d], dst_ref=buf.at[d],
            send_sem=send.at[way, d // 2], recv_sem=recv.at[d],
            device_id=device, device_id_type=MESH)

    def arrived(which, d):
        copy(which, d, SIB, sibling).wait_recv()

    def up_down(which, i, d, wait=False, own=False):
        def go(way, f):
            one = copy(which, d, way, z_side(f), own=own)
            one.wait_send() if wait else one.start()

        if i == 0:
            @pl.when(zz == 0)
            def _():
                go(ZU, 1)

        @pl.when(zz == 1)
        def _():
            if i == 0:
                go(ZU, 2)
                go(ZD, 0)
            else:
                go(ZU if i == 1 else ZD, 2 if i == 1 else 0)

    def relay(i, dy, dx):
        @pl.when(zz == 1)
        def _():
            d = shard(plane(i), dy, dx)
            for which in (K, V):
                arrived(which, d)
                copy(which, d, ZD, z_side(0)).start()

    def arrived_unless_relayed(which, d):
        @pl.when(zz == 0)
        def _():
            arrived(which, d)

    def first(i):
        a = shard(plane(i), 0, 0)
        own = i == 0
        meet = arrived if i == 1 else arrived_unless_relayed
        if not own:
            meet(K, a)
        copy(K, a, YS, y_side, own).start()
        if i < 2:
            up_down(K, i, a, own=own)
        if not own:
            meet(V, a)
        copy(V, a, XS, x_side, own).start()
        if i < 2:
            up_down(V, i, a, own=own)
        copy(K, a, XS, x_side, own).start()
        copy(V, a, YS, y_side, own).start()
        copy(K, a, SIB, sibling, own).start()
        copy(V, a, SIB, sibling, own).start()

    def second(i):
        p = plane(i)
        b, d = shard(p, 1, 0), shard(p, 0, 1)
        arrived(K, b)
        if i in (0, 3):
            copy(K, b, XS, x_side).start()
        arrived(V, d)
        if i in (0, 3):
            copy(V, d, YS, y_side).start()
        copy(K, b, SIB, sibling).start()
        copy(V, d, SIB, sibling).start()

    def third(i):
        p = plane(i)
        k_d, v_d = shard(p, 0, 1), shard(p, 1, 0)
        arrived(K, k_d)
        copy(K, k_d, SIB, sibling).start()
        arrived(V, v_d)
        copy(V, v_d, SIB, sibling).start()

    def fourth(i):
        d = shard(plane(i), 1, 1)
        for which in (K, V):
            (arrived_unless_relayed if i == 2 else arrived)(which, d)
            if i == 0:
                up_down(which, i, d)
        for which in (K, V):
            copy(which, d, SIB, sibling).start()

    def from_sibling(chunk):
        for i, dy, dx in chunk:
            arrived(K, shard(plane(i), dy, dx, 1))
            arrived(V, shard(plane(i), dy, dx, 1))

    def prepare(chunk):
        for j, (i, dy, dx) in enumerate(chunk):
            fill_bias(bias_ref, j, order_ref, shard(plane(i), dy, dx) // 2, pos, begin,
                      block_length)

    def compute(chunk, lo, hi_, last=False):
        pairs = [shard(plane(i), dy, dx) // 2 * 2 for i, dy, dx in chunk]

        def load(buf, g):
            return jnp.concatenate([
                buf[pl.ds(d, 2), :, head_columns(g)].reshape(2 * rows, HEAD_WIDTH)
                for d in pairs
            ], axis=0)

        @pl.loop(lo, hi_, step=2)
        def _(first_g):
            gs = [first_g + j for j in range(2)]
            attend(gs, [load(k_buf, g) for g in gs], [load(v_buf, g) for g in gs],
                   qt_ref, bias_ref, top_ref, total_ref, accum_ref)
            if last:
                for g in gs:
                    finish(g, out_ref, total_ref, accum_ref, rows, ratio)

    def near(i):
        return [(i, 0, 0), (i, 1, 0), (i, 0, 1)]

    def far(i):
        return [(i, 1, 1)]

    first(0)
    own_lengths.wait()
    own_order.wait()
    pos, begin = query_limits(lengths_ref, order_ref, me * rows, rows, block_length)
    reset(top_ref, total_ref, accum_ref)
    own_q.wait()
    pl.loop(0, groups)(lambda g: stack_queries(g, q_ref, qt_ref, ratio))
    second(0)
    first(1)
    relay(2, 0, 0)
    third(0)
    fourth(0)
    own_k.wait()
    own_v.wait()
    go = functools.partial
    steps = [
        (near(0) + far(0), [go(second, 1), go(first, 2), go(relay, 3, 0, 0), go(third, 1)]),
        (near(1), [go(second, 2), go(first, 3), go(relay, 2, 1, 1), go(third, 2)]),
        (near(2), [go(second, 3), go(fourth, 1), go(third, 3)]),
        (near(3) + far(1), [go(fourth, 2), go(fourth, 3)]),
        (far(2) + far(3), []),
    ]
    for n, (chunk, events) in enumerate(steps):
        from_sibling(chunk)
        prepare(chunk)
        done = 0
        for event in events:
            compute(chunk, done, done + 2)
            done += 2
            event()
        if done < groups:
            compute(chunk, done, groups, last=n == len(steps) - 1)

    for i in range(4):
        p = plane(i)
        a, b, d, e = shard(p, 0, 0), shard(p, 1, 0), shard(p, 0, 1), shard(p, 1, 1)
        for which, extra in ((K, (b, XS, x_side)), (V, (d, YS, y_side))):
            copy(which, a, XS, x_side).wait_send()
            copy(which, a, YS, y_side).wait_send()
            if i in (0, 3):
                copy(which, *extra).wait_send()
            up_down(which, i, a, wait=True)
            if i in (0, 2):
                up_down(which, i, e, wait=True)
            for s in (a, b, d, e):
                copy(which, s, SIB, sibling).wait_send()


def body(relayed, queries, keys, values, doc_lengths, stored_block_order):
    rows = queries.shape[0]
    groups = keys.shape[1] // HEAD_WIDTH
    ratio = queries.shape[1] // keys.shape[1]
    devices = lax.axis_size("blk") * lax.axis_size("head")
    block_length = rows * devices // stored_block_order.shape[0]
    chunk = max(512, block_length)
    scratch = [
        pltpu.VMEM((groups, HEAD_WIDTH, ratio * rows), BF16),
        pltpu.VMEM((chunk, LANES), F32),
        pltpu.VMEM((groups, 1, ratio * rows), F32),
        pltpu.VMEM((groups, 1, ratio * rows), F32),
        pltpu.VMEM((groups, HEAD_WIDTH, ratio * rows), F32),
    ]
    smem = pl.BlockSpec(memory_space=pltpu.SMEM)
    out_shape = jax.ShapeDtypeStruct(queries.shape, BF16)
    if relayed:
        gathered = pltpu.VMEM((devices, rows, keys.shape[1]), BF16)
        return pl.pallas_call(
            functools.partial(gather_kernel, ratio, block_length),
            out_shape=out_shape,
            in_specs=[pl.BlockSpec(memory_space=pltpu.HBM)] * 5,
            out_specs=pl.BlockSpec(memory_space=pltpu.VMEM),
            scratch_shapes=[pltpu.SMEM(doc_lengths.shape, jnp.int32),
                            pltpu.SMEM(stored_block_order.shape, jnp.int32),
                            pltpu.VMEM(queries.shape, BF16), gathered, gathered] + scratch + [
                pltpu.SemaphoreType.DMA((5,)),
                pltpu.SemaphoreType.DMA((devices,)),
                pltpu.SemaphoreType.DMA((devices,)),
                pltpu.SemaphoreType.DMA((5, devices // 2)),
                pltpu.SemaphoreType.DMA((5, devices // 2)),
            ],
            compiler_params=pltpu.CompilerParams(
                collective_id=0, has_side_effects=True, vmem_limit_bytes=48 << 20),
        )(doc_lengths, stored_block_order, queries, keys, values)
    keys = lax.all_gather(keys, ("blk", "head"), axis=0, tiled=True)
    values = lax.all_gather(values, ("blk", "head"), axis=0, tiled=True)
    first_row = (lax.axis_index("blk") * lax.axis_size("head") + lax.axis_index("head")) * rows
    whole = pl.BlockSpec(queries.shape, lambda i: (0, 0))
    part = pl.BlockSpec((chunk, keys.shape[1]), lambda i: (i, 0))
    return pl.pallas_call(
        functools.partial(chunk_kernel, ratio, block_length),
        out_shape=out_shape,
        grid=(keys.shape[0] // chunk,),
        in_specs=[smem, smem, smem, whole, part, part],
        out_specs=whole,
        scratch_shapes=scratch,
        compiler_params=pltpu.CompilerParams(vmem_limit_bytes=48 << 20),
    )(first_row.reshape(1), doc_lengths, stored_block_order, queries, keys, values)


def solution(mesh):
    rows = P(("blk", "head"), None)
    relayed = mesh.shape["blk"] == 8 and mesh.shape["head"] == 4
    return jax.shard_map(
        functools.partial(body, relayed), mesh=mesh,
        in_specs=(rows, rows, rows, P(), P()), out_specs=rows, check_vma=False)
```
